128 devices in a mesh: blk: 32 (over y, x_lo, z), vir: 4 (over x_hi, core).
Axes of the slice: x: 4 (x_hi: 2, x_lo: 2; x = x_hi * 2 + x_lo), y: 4, z: 4, core: 2. Of those that a mesh axis runs over, the one named last changes fastest.
Arguments:
- cholesky: float32 [8, 1536, 1536], P(None, 'blk', 'vir'), may hold values from -0.09375 to 0.09375
- amplitudes: float32 [8, 1536, 1536], P(None, 'blk', 'vir'), may hold values from -6 to 6
Outputs:
- ladder: float32 [8, 1536, 1536], P(None, 'vir', 'blk')
The draws below stay inside these ranges and needn't reach their ends.
All inputs are finite; a program needn't handle non-finite values.
Results may differ from the reference program's by a relative error of at most 0.0001.
Values sent between devices are 32-bit elements; how exact they have to be, the bound alone decides.
No kernel may reach another device: no remote copies, remote signals or barrier semaphores. Data moves between devices by JAX's collectives and lax.ppermute only.
A program may use at most 128 MiB of HBM per device.

```python
import jax
import jax.numpy as jnp
from jax import lax

V = 1536
NCHOL = 8
NPAIR = 8


def shard_levels(key, shape, split, least, high):
    factor_of, own = 1.0, jax.random.fold_in(key, 6)
    for axis_at, shards_of in split:
        heights = jnp.exp(jax.random.uniform(jax.random.fold_in(own, axis_at), (shards_of,), jnp.float32, least / len(split), high / len(split)))
        factor_of = factor_of * jnp.repeat(heights, shape[axis_at] // shards_of).reshape([-1 if axis == axis_at else 1 for axis in range(len(shape))])
    return factor_of


def scatter_about(stream_key, extent, scale, reach, split=(), held_as=jnp.bfloat16):
    entries = jax.random.normal(stream_key, extent, jnp.float32) * scale
    if len(split) > 0:
        entries = shard_levels(stream_key, extent, split, -0.22, 0.18) * entries
    return jnp.clip(entries, min=-reach, max=reach).astype(held_as)


def setup_inputs(seed: int = 0) -> dict:
    streams_of = jax.random.split(jax.random.key(seed), 3)
    return {
        "cholesky": scatter_about(streams_of[0], (NCHOL, V, V), (3 * V) ** -0.5, 0.09375, ((1, 32), (2, 4)), jnp.float32),
        "amplitudes": scatter_about(streams_of[1], (NPAIR, V, V), 1.0, 6.0, ((1, 32), (2, 4)), jnp.float32),
    }


def reference(cholesky, amplitudes):
    def one_vector(total, vector):
        halfway = jnp.einsum("bd,icd->ibc", vector, amplitudes, precision=lax.Precision.HIGHEST)
        total = total + jnp.einsum("ac,ibc->iab", vector, halfway, precision=lax.Precision.HIGHEST)
        return total, None

    start_total = jnp.zeros((NPAIR, V, V), jnp.float32)
    ladder, _ = lax.scan(one_vector, start_total, cholesky)
    return ladder
```

```python
import jax
import jax.numpy as jnp
from jax import lax
from jax.experimental import pallas as pl
from jax.experimental.pallas import tpu as pltpu
from jax.sharding import Mesh
from jax.sharding import PartitionSpec as P

AXES = ("y", "xl", "z", "xh", "c")
SIZES = (4, 2, 4, 2, 2)
F32, BF16 = jnp.float32, jnp.bfloat16


def coords(index):
    out = []
    for size in reversed(SIZES):
        out.append(index % size)
        index //= size
    return tuple(reversed(out))


def index_of(at):
    index = 0
    for size, value in zip(SIZES, at):
        index = index * size + value
    return index


def permute(value, target):
    pairs = [(s, index_of(target(*coords(s)))) for s in range(128)]
    return lax.ppermute(value, AXES, pairs)


def shift_x(at, by):
    y, xl, z, xh, c = at
    x = (2 * xh + xl + by) % 4
    return (y, x % 2, z, x // 2, c)


def shift_z(at, by):
    y, xl, z, xh, c = at
    return (y, xl, (z + by) % 4, xh, c)


def shift_y(at, by):
    y, xl, z, xh, c = at
    return ((y + by) % 4, xl, z, xh, c)


def near(at, by):
    return shift_z(at, by) if at[4] == 0 else shift_x(at, by)


def far(at, by):
    return shift_x(at, by) if at[4] == 0 else shift_z(at, by)


def swapped(at):
    y, xl, z, xh, c = at
    return (y, c, z, xh, xl)


def other_core(*at):
    return at[:4] + (1 - at[4],)


def split(value):
    high = value.astype(BF16)
    return high, (value - high.astype(F32)).astype(BF16)


def dot3(a, b):
    def one(p, q):
        return lax.dot_general(p, q, (((1,), (1,)), ((), ())), preferred_element_type=F32)

    return one(a[0], b[0]) + (one(a[0], b[1]) + one(a[1], b[0]))


def kernel(place, *refs):
    rows, (g, ga, fw, gb, fb) = refs[:8], refs[8:13]
    outs = refs[13:21]
    (l_rows, t_raw, l_cols, t_hi, t_lo, c_hi, c_lo, half, a_hi, a_lo, total, row_sem, t_sem, c_sem, out_sem) = refs[21:]
    y, z, x, c = place[0], place[1], place[2], place[3]

    def spot(u, v):
        on_first = c == 0
        at_z = lax.rem(z + jnp.where(on_first, u, v), 4)
        at_x = lax.rem(x + jnp.where(on_first, v, u), 4)
        return at_z, at_x

    t_copies, c_copies, row_copies = [], [], []
    down = jnp.where(c == 0, lax.rem(y + 3, 4), lax.rem(y + 1, 4))
    up = jnp.where(c == 0, lax.rem(y + 1, 4), lax.rem(y + 3, 4))
    across = lax.rem(y + 2, 4)
    for ref, at_y, core in ((g, y, c), (ga, down, c), (fw, across, c), (gb, up, 1 - c), (fb, across, 1 - c)):
        for k in range(ref.shape[0] // 2):
            core_k = core if k == 0 else 1 - core
            t_copies.append(
                pltpu.make_async_copy(
                    ref.at[2 * k],
                    t_raw.at[:, pl.ds(pl.multiple_of(lax.rem(at_y, 2) * 48, 48), 48), pl.ds(pl.multiple_of((2 * (at_y // 2) + core_k) * 384, 384), 384)],
                    t_sem,
                )
            )
            c_copies.append(
                pltpu.make_async_copy(
                    ref.at[2 * k + 1],
                    l_cols.at[pl.ds(at_y * 8, 8), :, pl.ds(pl.multiple_of(core_k * 384, 384), 384)],
                    c_sem,
                )
            )
    for ref, (v, u0) in zip(rows, ((0, 0), (0, 2), (1, 0), (1, 2), (3, 0), (3, 2), (2, 0), (2, 2))):
        for k in range(2):
            at_z, at_x = spot(u0 + k, v)
            row_copies.append(
                pltpu.make_async_copy(
                    ref.at[k],
                    l_rows.at[:, pl.ds(pl.multiple_of(at_z * 48, 48), 48), pl.ds(pl.multiple_of(at_x * 384, 384), 384)],
                    row_sem,
                )
            )
    for copy in t_copies + row_copies + c_copies:
        copy.start()
    for copy in t_copies:
        copy.wait()

    @pl.loop(0, 8)
    def _(i):
        high, low = split(t_raw[i])
        t_hi[pl.ds(pl.multiple_of(i * 96, 96), 96), :] = high
        t_lo[pl.ds(pl.multiple_of(i * 96, 96), 96), :] = low

    for copy in row_copies:
        copy.wait()

    @pl.loop(0, 8)
    def _(p):
        b = split(l_rows[p])
        for m in range(2):
            chunk = pl.ds(m * 384, 384)
            h = dot3((t_hi[chunk, :], t_lo[chunk, :]), b)
            for j in range(8):
                i, lo = m * 4 + j // 2, j % 2
                half[i, pl.ds(pl.multiple_of((lo * 8 + p) * 48, 48), 48), :] = h[j * 48 : (j + 1) * 48, :]

    @pl.loop(0, 8)
    def _(i):
        high, low = split(half[i].T)
        a_hi[pl.ds(pl.multiple_of(i * 192, 192), 192), :] = high
        a_lo[pl.ds(pl.multiple_of(i * 192, 192), 192), :] = low

    for copy in c_copies:
        copy.wait()

    @pl.loop(0, 8)
    def _(e):
        high, low = split(l_cols[pl.ds(e * 4, 4)].reshape(192, 768))
        c_hi[pl.ds(pl.multiple_of(e * 192, 192), 192), :] = high
        c_lo[pl.ds(pl.multiple_of(e * 192, 192), 192), :] = low

    for n in range(2):
        wide = pl.ds(n * 768, 768)

        @pl.loop(0, 4)
        def _(m):
            chunk = pl.ds(pl.multiple_of(m * 384, 384), 384)
            r = dot3((a_hi[chunk, :], a_lo[chunk, :]), (c_hi[wide, :], c_lo[wide, :]))
            for j in range(2):
                for at_z in range(4):
                    for k in range(2):
                        to_z = lax.rem(at_z - z + 4, 4)
                        to_x = lax.rem(n * 2 + k - x + 4, 4)
                        v = jnp.where(c == 0, to_x, to_z)
                        u = jnp.where(c == 0, to_z, to_x)
                        rows_at = j * 192 + at_z * 48
                        total[v * 4 + u, m * 2 + j] = r[rows_at : rows_at + 48, k * 384 : (k + 1) * 384]

    copies = []
    for k, out in enumerate(outs):
        copies.append(pltpu.make_async_copy(total.at[pl.ds(2 * k, 2)], out, out_sem))
    for copy in copies:
        copy.start()
    for copy in copies:
        copy.wait()


def multiply(place, rows, cols):
    piece = jax.ShapeDtypeStruct((2, 8, 48, 384), F32)
    anywhere = pl.BlockSpec(memory_space=pl.ANY)
    return pl.pallas_call(
        kernel,
        out_shape=[piece] * 8,
        in_specs=[pl.BlockSpec(memory_space=pltpu.SMEM)] + [anywhere] * 13,
        out_specs=[anywhere] * 8,
        scratch_shapes=[
            pltpu.VMEM((8, 192, 1536), F32),
            pltpu.VMEM((8, 96, 1536), F32),
            pltpu.VMEM((32, 48, 768), F32),
            pltpu.VMEM((768, 1536), BF16),
            pltpu.VMEM((768, 1536), BF16),
            pltpu.VMEM((1536, 768), BF16),
            pltpu.VMEM((1536, 768), BF16),
            pltpu.VMEM((8, 768, 192), F32),
            pltpu.VMEM((1536, 768), BF16),
            pltpu.VMEM((1536, 768), BF16),
            pltpu.VMEM((16, 8, 48, 384), F32),
            pltpu.SemaphoreType.DMA,
            pltpu.SemaphoreType.DMA,
            pltpu.SemaphoreType.DMA,
            pltpu.SemaphoreType.DMA,
        ],
        compiler_params=pltpu.CompilerParams(vmem_limit_bytes=56 << 20),
        cost_estimate=pl.CostEstimate(flops=3 * 7247757312, bytes_accessed=28 << 20, transcendentals=0),
    )(place, *rows, *cols)


def body(cholesky, amplitudes):
    y, xl, z, xh, c = (lax.axis_index(axis) for axis in AXES)
    place = jnp.stack([y, z, 2 * xh + xl, c]).astype(jnp.int32)

    near_rows = [permute(cholesky, lambda *at, u=u: near(swapped(at), -u)) for u in range(4)]
    s01, s23 = jnp.stack(near_rows[:2]), jnp.stack(near_rows[2:])

    def from_plus(value):
        return permute(value, lambda *at: far(at, -1))

    def from_minus(value):
        return permute(value, lambda *at: far(at, 1))

    p01, m23 = from_plus(s01), from_minus(s23)
    p23, m01 = from_plus(s23), from_minus(s01)
    rows = (s01, s23, p01, p23, m01, m23, from_plus(p01), from_minus(m23))

    own_t = permute(amplitudes, lambda y, xl, z, xh, c: (2 * xh + y % 2, xl, z, y // 2, c))
    columns = cholesky.reshape(8, 48, 8, 48).transpose(2, 1, 0, 3).reshape(8, 48, 384)
    own_c = lax.all_to_all(columns, ("xl", "z"), 0, 0, tiled=True)
    own = jnp.stack([own_t, own_c])
    g = jnp.concatenate([own, permute(own, other_core)])

    def along_y(value):
        return permute(value, lambda *at: shift_y(at, 1 if at[4] == 0 else -1))

    ga = along_y(g)
    fw = along_y(ga[:2])
    cols = (g, ga, fw, permute(ga, other_core), permute(fw, other_core))

    r0a, r0b, r1a, r1b, r2a, r2b, r3a, r3b = multiply(place, rows, cols)

    def to_plus(value):
        return permute(value, lambda *at: far(at, 1))

    def to_minus(value):
        return permute(value, lambda *at: far(at, -1))

    a0, a1 = to_plus(r2a), to_minus(r2b)
    b1, d0 = to_plus(r1b), to_minus(r3a)
    b0, d1 = to_plus(r1a + a0), to_minus(r3b + a1)
    q = (r0a + b0 + d0, r0b + b1 + d1)
    pieces = [q[u // 2][u % 2] for u in range(4)]
    got = [permute(piece, lambda *at, u=u: swapped(near(at, u))) for u, piece in enumerate(pieces)]
    return ((got[0] + got[1]) + (got[2] + got[3])).transpose(0, 2, 1)


def solution(mesh):
    fine = Mesh(mesh.devices.reshape(SIZES), AXES)
    split_in = P(None, ("y", "xl", "z"), ("xh", "c"))
    return jax.shard_map(
        body, mesh=fine, in_specs=(split_in, split_in), out_specs=P(None, ("xh", "c"), ("y", "xl", "z")), check_vma=False
    )
```

```python
import functools

import jax
import jax.numpy as jnp
from jax import lax
from jax.experimental import pallas as pl
from jax.experimental.pallas import tpu as pltpu
from jax.sharding import Mesh
from jax.sharding import PartitionSpec as P

AXES = ("y", "xl", "z", "xh", "c")
SIZES = (4, 2, 4, 2, 2)
F32, BF16 = jnp.float32, jnp.bfloat16


def coords(index):
    out = []
    for size in reversed(SIZES):
        out.append(index % size)
        index //= size
    return tuple(reversed(out))


def index_of(at):
    index = 0
    for size, value in zip(SIZES, at):
        index = index * size + value
    return index


def permute(value, target):
    pairs = [(s, index_of(target(*coords(s)))) for s in range(128)]
    return lax.ppermute(value, AXES, pairs)


def shift_x(at, by):
    y, xl, z, xh, c = at
    x = (2 * xh + xl + by) % 4
    return (y, x % 2, z, x // 2, c)


def shift_z(at, by):
    y, xl, z, xh, c = at
    return (y, xl, (z + by) % 4, xh, c)


def shift_y(at, by):
    y, xl, z, xh, c = at
    return ((y + by) % 4, xl, z, xh, c)


def near(at, by):
    return shift_z(at, by) if at[4] == 0 else shift_x(at, by)


def far(at, by):
    return shift_x(at, by) if at[4] == 0 else shift_z(at, by)


def swapped(at):
    y, xl, z, xh, c = at
    return (y, c, z, xh, xl)


def other_core(*at):
    return at[:4] + (1 - at[4],)


def split(value):
    high = value.astype(BF16)
    return high, (value - high.astype(F32)).astype(BF16)


def dot3(a, b):
    def one(p, q):
        return lax.dot_general(p, q, (((1,), (1,)), ((), ())), preferred_element_type=F32)

    return one(a[0], b[0]) + (one(a[0], b[1]) + one(a[1], b[0]))


def offset(value, size):
    return pl.ds(pl.multiple_of(value * size, size), size)


def row_copies(place, refs, target, vectors, sem):
    z, x, c = place[1], place[2], place[3]
    copies = []
    for ref, v, us in zip(refs, (0, 1, 3, 2, 2), (range(4), range(4), range(4), range(2), range(2, 4))):
        for k, u in enumerate(us):
            at_z = lax.rem(z + jnp.where(c == 0, u, v), 4)
            at_x = lax.rem(x + jnp.where(c == 0, v, u), 4)
            place_of = target.at[vectors, offset(at_z, 48), offset(at_x, 384)]
            copies.append(pltpu.make_async_copy(ref.at[k, vectors], place_of, sem))
    return copies


def shuffle_kernel(l_ref, out):
    for m in range(8):
        out[m] = jnp.concatenate([l_ref[p][:, m * 48 : m * 48 + 48] for p in range(8)], axis=1)


def start(copies):
    for copy in copies:
        copy.start()


def wait(copies):
    for copy in copies:
        copy.wait()


def ladder_of(place, offsets, a_hi, a_lo, c_hi, c_lo, outs):
    z, x, c = place[1], place[2], place[3]
    for n, v in enumerate(offsets):
        for k, out in enumerate(outs[2 * n : 2 * n + 2]):

            @pl.loop(0, 2)
            def _(w):
                u = 2 * k + w
                at_z = lax.rem(z + jnp.where(c == 0, u, v), 4)
                at_x = lax.rem(x + jnp.where(c == 0, v, u), 4)
                r = dot3((a_hi[at_z], a_lo[at_z]), (c_hi[at_x], c_lo[at_x]))
                out[w] = r.reshape(8, 48, 384)


def second_kernel(place, *refs):
    rows, amps, columns = refs[:5], refs[5:7], refs[7:9]
    out_a, out_b, a_hi, a_lo, c_hi, c_lo = refs[9:15]
    l_rows, t_raw, t_hi, t_lo, half, l_cols, t_sem, row_sem, c_sem = refs[15:]
    y, c = place[0], place[3]
    t_copies, c_copies = [], []
    for k in range(4):
        at_y = lax.rem(y + k, 4)
        for ref, core in zip(amps, (c, 1 - c)):
            target = t_raw.at[:, offset(lax.rem(at_y, 2), 48), offset(at_y // 2 * 2 + core, 384)]
            t_copies.append(pltpu.make_async_copy(ref.at[k], target, t_sem))
        for ref, core in zip(columns, (c, 1 - c)):
            c_copies.append(pltpu.make_async_copy(ref.at[k], l_cols.at[at_y, :, :, offset(core, 384)], c_sem))
    quads = [pl.ds(4 * q, 4) for q in range(2)]
    r_copies = [row_copies(place, rows, l_rows, quads[q], row_sem.at[q]) for q in range(2)]
    start(t_copies + r_copies[0] + r_copies[1] + c_copies)
    wait(t_copies)

    @pl.loop(0, 8)
    def _(i):
        high, low = split(t_raw[i])
        t_hi[offset(i, 96), :] = high
        t_lo[offset(i, 96), :] = low

    for q in range(2):
        wait(r_copies[q])
        b = split(l_rows[quads[q]].reshape(768, 1536))
        for m in range(2):
            chunk = pl.ds(m * 384, 384)
            h = dot3((t_hi[chunk, :], t_lo[chunk, :]), b)
            for j in range(8):
                for p in range(4):
                    at = ((j % 2) * 8 + q * 4 + p) * 48
                    half[m * 4 + j // 2, at : at + 48, :] = h[j * 48 : j * 48 + 48, p * 192 : p * 192 + 192]

    @pl.loop(0, 8)
    def _(i):
        high, low = split(half[i].T)
        for at_z in range(4):
            a_hi[at_z, offset(i, 48), :] = high[at_z * 48 : at_z * 48 + 48, :]
            a_lo[at_z, offset(i, 48), :] = low[at_z * 48 : at_z * 48 + 48, :]

    wait(c_copies)

    @pl.loop(0, 4)
    def _(e):
        c_hi[e], c_lo[e] = split(l_cols[e].reshape(384, 768))

    ladder_of(place, (2,), a_hi, a_lo, c_hi, c_lo, (out_a, out_b))


def third_kernel(offsets, place, a_hi, a_lo, c_hi, c_lo, *outs):
    ladder_of(place, offsets, a_hi, a_lo, c_hi, c_lo, outs)


ANYWHERE = pl.BlockSpec(memory_space=pl.ANY)
ON_SMEM = pl.BlockSpec(memory_space=pltpu.SMEM)
ON_VMEM = pl.BlockSpec(memory_space=pltpu.VMEM)
DMA = pltpu.SemaphoreType.DMA
BLOCKS = (4, 384, 768)
PAIR = jax.ShapeDtypeStruct((2, 8, 48, 384), F32)
HALF = jax.ShapeDtypeStruct(BLOCKS, BF16)


def call(body, out_shape, spec, scratch, megabytes, units, place, *args):
    return pl.pallas_call(
        body,
        out_shape=out_shape,
        in_specs=[ON_SMEM] + [spec] * len(args),
        out_specs=[ON_VMEM] * len(out_shape),
        scratch_shapes=scratch,
        compiler_params=pltpu.CompilerParams(vmem_limit_bytes=megabytes << 20),
        cost_estimate=pl.CostEstimate(flops=units * 3 * 905969664, bytes_accessed=12 << 20, transcendentals=0),
    )(place, *args)


def second(place, rows, amps, columns):
    scratch = [
        pltpu.VMEM((8, 192, 1536), F32),
        pltpu.VMEM((8, 96, 1536), F32),
        pltpu.VMEM((768, 1536), BF16),
        pltpu.VMEM((768, 1536), BF16),
        pltpu.VMEM((8, 768, 192), F32),
        pltpu.VMEM((4, 8, 48, 768), F32),
        DMA,
        DMA((2,)),
        DMA,
    ]
    return call(second_kernel, [PAIR, PAIR] + [HALF] * 4, ANYWHERE, scratch, 56, 5, place, *rows, *amps, *columns)


def third(offsets, place, halves):
    body = functools.partial(third_kernel, offsets)
    return call(body, [PAIR] * (2 * len(offsets)), ON_VMEM, [], 24, len(offsets), place, *halves)


def shuffle(cholesky):
    return pl.pallas_call(
        shuffle_kernel,
        out_shape=jax.ShapeDtypeStruct((8, 48, 384), F32),
        in_specs=[ON_VMEM],
        out_specs=ON_VMEM,
        compiler_params=pltpu.CompilerParams(vmem_limit_bytes=8 << 20),
    )(cholesky)


def body(cholesky, amplitudes):
    y, xl, z, xh, c = (lax.axis_index(axis) for axis in AXES)
    place = jnp.stack([y, z, 2 * xh + xl, c]).astype(jnp.int32)

    def from_plus(value):
        return permute(value, lambda *at: far(at, -1))

    def from_minus(value):
        return permute(value, lambda *at: far(at, 1))

    mine = permute(cholesky, lambda *at: swapped(at))
    near_rows = [mine] + [permute(mine, lambda *at, u=u: near(at, -u)) for u in (1, 2, 3)]

    own_t = permute(amplitudes, lambda y, xl, z, xh, c: (2 * xh + y % 2, xl, z, y // 2, c))
    columns, mine = lax.optimization_barrier((shuffle(cholesky), mine))
    own_c = lax.all_to_all(columns, ("xl", "z"), 0, 0, tiled=True)

    def round_y(own):
        ring = jnp.stack([own] + [permute(own, lambda *at, k=k: shift_y(at, -k)) for k in (1, 2, 3)])
        return ring, permute(ring, other_core)

    amps, cols = round_y(own_t), round_y(own_c)

    s = jnp.stack(near_rows)
    p, m = from_plus(s), from_minus(s)
    rows = (s, p, m, from_plus(p[:2]), from_minus(m[2:]))

    r2a, r2b, *halves = second(place, rows, amps, cols)
    r1a, r1b, r3a, r3b = third((1, 3), place, halves)
    r0a, r0b = third((0,), place, halves)

    def to_plus(value):
        return permute(value, lambda *at: far(at, 1))

    def to_minus(value):
        return permute(value, lambda *at: far(at, -1))

    a0, a1 = to_plus(r2a), to_minus(r2b)
    b1, d0 = to_plus(r1b), to_minus(r3a)
    b0, d1 = to_plus(r1a + a0), to_minus(r3b + a1)
    q = (r0a + b0 + d0, r0b + b1 + d1)
    got = [permute(q[u // 2][u % 2], lambda *at, u=u: near(at, u)) for u in (1, 2, 3)]
    total = (q[0][0] + got[0]) + (got[1] + got[2])
    return permute(total, lambda *at: swapped(at)).transpose(0, 2, 1)


def solution(mesh):
    fine = Mesh(mesh.devices.reshape(SIZES), AXES)
    split_in = P(None, ("y", "xl", "z"), ("xh", "c"))
    return jax.shard_map(
        body, mesh=fine, in_specs=(split_in, split_in), out_specs=P(None, ("xh", "c"), ("y", "xl", "z")), check_vma=False
    )
```

```python
import functools

import jax
import jax.numpy as jnp
from jax import lax
from jax.experimental import pallas as pl
from jax.experimental.pallas import tpu as pltpu
from jax.sharding import Mesh
from jax.sharding import PartitionSpec as P

AXES = ("y", "xl", "z", "xh", "c")
SIZES = (4, 2, 4, 2, 2)
F32, BF16 = jnp.float32, jnp.bfloat16


def coords(index):
    out = []
    for size in reversed(SIZES):
        out.append(index % size)
        index //= size
    return tuple(reversed(out))


def index_of(at):
    index = 0
    for size, value in zip(SIZES, at):
        index = index * size + value
    return index


def permute(value, target):
    pairs = [(s, index_of(target(*coords(s)))) for s in range(128)]
    return lax.ppermute(value, AXES, pairs)


def shift_x(at, by):
    y, xl, z, xh, c = at
    x = (2 * xh + xl + by) % 4
    return (y, x % 2, z, x // 2, c)


def shift_z(at, by):
    y, xl, z, xh, c = at
    return (y, xl, (z + by) % 4, xh, c)


def shift_y(at, by):
    y, xl, z, xh, c = at
    return ((y + by) % 4, xl, z, xh, c)


def near(at, by):
    return shift_z(at, by) if at[4] == 0 else shift_x(at, by)


def far(at, by):
    return shift_x(at, by) if at[4] == 0 else shift_z(at, by)


def swapped(at):
    y, xl, z, xh, c = at
    return (y, xl, z // 2 * 2 + c, xh, z % 2)


def other_core(*at):
    return at[:4] + (1 - at[4],)


def split(value):
    high = value.astype(BF16)
    return high, (value - high.astype(F32)).astype(BF16)


def dot3(a, b):
    def one(p, q):
        return lax.dot_general(p, q, (((1,), (1,)), ((), ())), preferred_element_type=F32)

    return one(a[0], b[0]) + (one(a[0], b[1]) + one(a[1], b[0]))


def offset(value, size):
    return pl.ds(pl.multiple_of(value * size, size), size)


def row_copies(place, refs, target, vectors, sem):
    z, x, c = place[1], place[2], place[3]
    copies = []
    for ref, v, us in zip(refs, (0, 1, 3, 2, 2), (range(4), range(4), range(4), range(2), range(2, 4))):
        for k, u in enumerate(us):
            at_z = lax.rem(z + jnp.where(c == 0, u, v), 4)
            at_x = lax.rem(x + jnp.where(c == 0, v, u), 4)
            b, d = lax.rem(at_x, 2) * 2 + at_z // 2, at_x // 2 * 2 + lax.rem(at_z, 2)
            copies.append(pltpu.make_async_copy(ref.at[k, vectors], target.at[vectors, offset(b, 48), offset(d, 384)], sem))
    return copies


def shuffle_kernel(l_ref, out):
    for m in range(8):
        out[m] = jnp.concatenate([l_ref[p][:, m * 48 : m * 48 + 48] for p in range(8)], axis=1)


def start(copies):
    for copy in copies:
        copy.start()


def wait(copies):
    for copy in copies:
        copy.wait()


def ladder_of(place, v, a_hi, a_lo, c_hi, c_lo, near_ones, far_ones):
    z, x, c = place[1], place[2], place[3]
    at_z, at_x = lax.rem(z + v, 4), lax.rem(x + v, 4)
    bs = [jnp.where(c == 0, lax.rem(at_x, 2) * 2 + k, at_z // 2 + 2 * k) for k in range(2)]
    cs = [jnp.where(c == 0, at_x // 2 * 2 + k, lax.rem(at_z, 2) + 2 * k) for k in range(2)]
    left = [jnp.concatenate([ref[b] for b in bs]) for ref in (a_hi, a_lo)]
    right = [jnp.concatenate([ref[b] for b in cs]) for ref in (c_hi, c_lo)]
    r = dot3(left, right)
    for i in range(2):
        for j in range(2):
            block = r[i * 384 : i * 384 + 384, j * 384 : j * 384 + 384].reshape(8, 48, 384)
            u = lax.rem(jnp.where(c == 0, 2 * i + j - z, 2 * j + i - x) + 4, 4)

            for n, ref in enumerate((near_ones, far_ones)):

                @pl.when(u // 2 == n)
                def _():
                    ref[lax.rem(u, 2)] = block


def halves_kernel(place, *refs):
    amps, columns, outs = refs[:2], refs[2:4], refs[4:8]
    t_raw, l_cols, t_hi, t_lo, c_hi, c_lo, t_sem, c_sem, out_sem = refs[8:]
    y, c = place[0], place[3]
    t_copies, c_copies = [], []
    for k in range(4):
        at_y = lax.rem(y + k, 4)
        for ref, core in zip(amps, (c, 1 - c)):
            target = t_raw.at[:, offset(lax.rem(at_y, 2), 48), offset(at_y // 2 * 2 + core, 384)]
            t_copies.append(pltpu.make_async_copy(ref.at[k], target, t_sem))
        for ref, core in zip(columns, (c, 1 - c)):
            c_copies.append(pltpu.make_async_copy(ref.at[k], l_cols.at[at_y, :, :, offset(core, 384)], c_sem))
    start(t_copies + c_copies)
    wait(t_copies)

    @pl.loop(0, 8)
    def _(i):
        t_hi[offset(i, 96), :], t_lo[offset(i, 96), :] = split(t_raw[i])

    wait(c_copies)

    @pl.loop(0, 4)
    def _(e):
        c_hi[e], c_lo[e] = split(l_cols[e].reshape(384, 768))

    copies = [pltpu.make_async_copy(ref, out, out_sem) for ref, out in zip((t_hi, t_lo, c_hi, c_lo), outs)]
    start(copies)
    wait(copies)


def second_kernel(place, *refs):
    rows, halves_in, outs = refs[:5], refs[5:9], refs[9:17]
    l_rows, t_hi, t_lo, c_hi, c_lo, half, a_hi, a_lo = refs[17:25]
    blocks, (t_sem, row_sem, c_sem, out_sem) = refs[25:31], refs[31:]
    t_copies = [pltpu.make_async_copy(halves_in[k], ref, t_sem) for k, ref in enumerate((t_hi, t_lo))]
    c_copies = [pltpu.make_async_copy(halves_in[2 + k], ref, c_sem) for k, ref in enumerate((c_hi, c_lo))]
    r_copies = [row_copies(place, rows, l_rows, pl.ds(4 * q, 4), row_sem.at[q]) for q in range(2)]
    start(t_copies + r_copies[0] + r_copies[1] + c_copies)
    wait(t_copies)
    for q in range(2):
        wait(r_copies[q])
        b = split(l_rows[4 * q : 4 * q + 4].reshape(768, 1536))
        for m in range(2):
            chunk = pl.ds(m * 384, 384)
            h = dot3((t_hi[chunk, :], t_lo[chunk, :]), b)
            for j in range(8):
                for p in range(4):
                    at = ((j % 2) * 8 + q * 4 + p) * 48
                    half[m * 4 + j // 2, at : at + 48, :] = h[j * 48 : j * 48 + 48, p * 192 : p * 192 + 192]

    @pl.loop(0, 8)
    def _(i):
        high, low = split(half[i].T)
        for b in range(4):
            a_hi[b, offset(i, 48), :] = high[b * 48 : b * 48 + 48, :]
            a_lo[b, offset(i, 48), :] = low[b * 48 : b * 48 + 48, :]

    wait(c_copies)
    copies = [pltpu.make_async_copy(ref, out, out_sem) for ref, out in zip((*blocks, a_hi, a_lo), outs)]
    start(copies[6:])
    for k, v in enumerate((2, 1, 3)):
        ladder_of(place, v, a_hi, a_lo, c_hi, c_lo, blocks[2 * k], blocks[2 * k + 1])
        start(copies[2 * k : 2 * k + 2])
    wait(copies)


def third_kernel(place, a_hi_in, a_lo_in, c_hi_in, c_lo_in, b1, d0, out_a, out_b, a_hi, a_lo, c_hi, c_lo, sem):
    del b1, d0
    pairs = ((a_hi_in, a_hi), (a_lo_in, a_lo), (c_hi_in, c_hi), (c_lo_in, c_lo))
    copies = [pltpu.make_async_copy(ref, held, sem) for ref, held in pairs]
    start(copies)
    wait(copies)
    ladder_of(place, 0, a_hi, a_lo, c_hi, c_lo, out_a, out_b)


ANYWHERE = pl.BlockSpec(memory_space=pl.ANY)
ON_HBM = pl.BlockSpec(memory_space=pltpu.HBM)
ON_SMEM = pl.BlockSpec(memory_space=pltpu.SMEM)
ON_VMEM = pl.BlockSpec(memory_space=pltpu.VMEM)
DMA = pltpu.SemaphoreType.DMA
BLOCKS = (4, 384, 768)
PAIR = jax.ShapeDtypeStruct((2, 8, 48, 384), F32)
HALF = jax.ShapeDtypeStruct(BLOCKS, BF16)


AMPS = (768, 1536)
HALF_AMPS = jax.ShapeDtypeStruct(AMPS, BF16)


def call(body, out_shape, out_spec, scratch, megabytes, units, place, *args):
    return pl.pallas_call(
        body,
        out_shape=out_shape,
        in_specs=[ON_SMEM] + [ANYWHERE] * len(args),
        out_specs=[out_spec] * len(out_shape),
        scratch_shapes=scratch,
        compiler_params=pltpu.CompilerParams(vmem_limit_bytes=megabytes << 20),
        cost_estimate=pl.CostEstimate(flops=units * 3 * 905969664, bytes_accessed=12 << 20, transcendentals=0),
    )(place, *args)


def halves(place, amps, columns):
    scratch = [pltpu.VMEM((8, 96, 1536), F32), pltpu.VMEM((4, 8, 48, 768), F32)]
    scratch += [pltpu.VMEM(AMPS, BF16)] * 2 + [pltpu.VMEM(BLOCKS, BF16)] * 2 + [DMA] * 3
    return call(halves_kernel, [HALF_AMPS] * 2 + [HALF] * 2, ON_HBM, scratch, 24, 1, place, *amps, *columns)


def second(place, rows, parts):
    scratch = [pltpu.VMEM((8, 192, 1536), F32)] + [pltpu.VMEM(AMPS, BF16)] * 2 + [pltpu.VMEM(BLOCKS, BF16)] * 2
    scratch += [pltpu.VMEM((8, 768, 192), F32)] + [pltpu.VMEM(BLOCKS, BF16)] * 2 + [pltpu.VMEM(PAIR.shape, F32)] * 6
    scratch += [DMA, DMA((2,)), DMA, DMA]
    return call(second_kernel, [PAIR] * 6 + [HALF] * 2, ON_HBM, scratch, 48, 7, place, *rows, *parts)


def third(place, parts, after):
    scratch = [pltpu.VMEM(BLOCKS, BF16)] * 4 + [DMA]
    return call(third_kernel, [PAIR] * 2, ON_VMEM, scratch, 24, 1, place, *parts, *after)


def shuffle(cholesky):
    return pl.pallas_call(
        shuffle_kernel,
        out_shape=jax.ShapeDtypeStruct((8, 48, 384), F32),
        in_specs=[ON_VMEM],
        out_specs=ON_VMEM,
        compiler_params=pltpu.CompilerParams(vmem_limit_bytes=8 << 20),
    )(cholesky)


def body(cholesky, amplitudes):
    y, xl, z, xh, c = (lax.axis_index(axis) for axis in AXES)
    place = jnp.stack([y, z, 2 * xh + xl, c]).astype(jnp.int32)

    def from_plus(value):
        return permute(value, lambda *at: far(at, -1))

    def from_minus(value):
        return permute(value, lambda *at: far(at, 1))

    mine = permute(cholesky, lambda *at: swapped(at))
    near_rows = [mine] + [permute(mine, lambda *at, u=u: near(at, -u)) for u in (1, 2, 3)]

    own_t = permute(amplitudes, lambda y, xl, z, xh, c: (2 * xh + y % 2, xl, z, y // 2, c))
    columns, mine = lax.optimization_barrier((shuffle(cholesky), mine))
    own_c = lax.all_to_all(columns, ("xl", "z"), 0, 0, tiled=True)

    def from_y(value, by):
        return permute(value, lambda *at: shift_y(at, -by))

    def round_y(own):
        p, m = from_y(own, 1), from_y(own, -1)
        far_one = jnp.concatenate([from_y(p[:4], 1), from_y(m[4:], -1)])
        ring = jnp.stack([own, p, far_one, m])
        return ring, permute(ring, other_core)

    amps, cols = round_y(own_t), round_y(own_c)

    s = jnp.stack(near_rows)
    p, m = from_plus(s), from_minus(s)
    rows = (s, p, m, from_plus(p[:2]), from_minus(m[2:]))

    t_hi, t_lo, c_hi, c_lo = halves(place, amps, cols)
    r2a, r2b, r1a, r1b, r3a, r3b, a_hi, a_lo = second(place, rows, (t_hi, t_lo, c_hi, c_lo))

    def to_plus(value):
        return permute(value, lambda *at: far(at, 1))

    def to_minus(value):
        return permute(value, lambda *at: far(at, -1))

    a0, a1 = to_plus(r2a), to_minus(r2b)
    b1, d0 = to_plus(r1b), to_minus(r3a)
    r0a, r0b = third(place, (a_hi, a_lo, c_hi, c_lo), (b1, d0))
    b0, d1 = to_plus(r1a + a0), to_minus(r3b + a1)
    q = (r0a + b0 + d0, r0b + b1 + d1)
    got = [permute(q[u // 2][u % 2], lambda *at, u=u: near(at, u)) for u in (1, 2, 3)]
    total = (q[0][0] + got[0]) + (got[1] + got[2])
    return permute(total, lambda *at: swapped(at)).transpose(0, 2, 1)


def solution(mesh):
    fine = Mesh(mesh.devices.reshape(SIZES), AXES)
    split_in = P(None, ("y", "xl", "z"), ("xh", "c"))
    return jax.shard_map(
        body, mesh=fine, in_specs=(split_in, split_in), out_specs=P(None, ("xh", "c"), ("y", "xl", "z")), check_vma=False
    )
```

```python
import functools

import jax
import jax.numpy as jnp
from jax import lax
from jax.experimental import pallas as pl
from jax.experimental.pallas import tpu as pltpu
from jax.sharding import Mesh
from jax.sharding import PartitionSpec as P

AXES = ("y", "xl", "z", "xh", "c")
SIZES = (4, 2, 4, 2, 2)
F32, BF16 = jnp.float32, jnp.bfloat16


def coords(index):
    out = []
    for size in reversed(SIZES):
        out.append(index % size)
        index //= size
    return tuple(reversed(out))


def index_of(at):
    index = 0
    for size, value in zip(SIZES, at):
        index = index * size + value
    return index


def permute(value, target):
    pairs = [(s, index_of(target(*coords(s)))) for s in range(128)]
    return lax.ppermute(value, AXES, pairs)


def shift_x(at, by):
    y, xl, z, xh, c = at
    x = (2 * xh + xl + by) % 4
    return (y, x % 2, z, x // 2, c)


def shift_z(at, by):
    y, xl, z, xh, c = at
    return (y, xl, (z + by) % 4, xh, c)


def shift_y(at, by):
    y, xl, z, xh, c = at
    return ((y + by) % 4, xl, z, xh, c)


def near(at, by):
    return shift_z(at, by) if at[4] == 0 else shift_x(at, by)


def far(at, by):
    return shift_x(at, by) if at[4] == 0 else shift_z(at, by)


def swapped(at):
    y, xl, z, xh, c = at
    return (y, xl, z // 2 * 2 + c, xh, z % 2)


def other_core(*at):
    return at[:4] + (1 - at[4],)


def split(value):
    high = value.astype(BF16)
    return high, (value - high.astype(F32)).astype(BF16)


def times(a, b):
    return lax.dot_general(a, b, (((1,), (1,)), ((), ())), preferred_element_type=F32)


def dot3(a, b):
    return times(a[0], b[0]) + (times(a[0], b[1]) + times(a[1], b[0]))


def offset(value, size):
    return pl.ds(pl.multiple_of(value * size, size), size)


def row_copies(place, refs, target, vectors, sem):
    z, x, c = place[1], place[2], place[3]
    copies = []
    for ref, v, us in zip(refs, (0, 1, 3, 2, 2), (range(4), range(4), range(4), range(2), range(2, 4))):
        for k, u in enumerate(us):
            at_z = lax.rem(z + jnp.where(c == 0, u, v), 4)
            at_x = lax.rem(x + jnp.where(c == 0, v, u), 4)
            b, d = lax.rem(at_x, 2) * 2 + at_z // 2, at_x // 2 * 2 + lax.rem(at_z, 2)
            copies.append(pltpu.make_async_copy(ref.at[k, vectors], target.at[vectors, offset(b, 48), offset(d, 384)], sem))
    return copies


def shuffle_kernel(l_ref, after, out):
    del after
    for m in range(8):
        out[m] = jnp.concatenate([l_ref[p][:, m * 48 : m * 48 + 48] for p in range(8)], axis=1)


def start(copies):
    for copy in copies:
        copy.start()


def wait(copies):
    for copy in copies:
        copy.wait()


def ladder_of(place, v, a_wide, c_wide, out):
    z, x, c = place[1], place[2], place[3]
    at_z, at_x = lax.rem(z + v, 4), lax.rem(x + v, 4)
    columns = [jnp.where(c == 0, at_x // 2 * 2 + j, lax.rem(at_z, 2) + 2 * j) for j in range(2)]
    for i in range(2):
        b = jnp.where(c == 0, lax.rem(at_x, 2) * 2 + i, at_z // 2 + 2 * i)
        r = times(a_wide[b], jnp.concatenate([c_wide[at] for at in columns]))
        for j in range(2):
            u = lax.rem(jnp.where(c == 0, 2 * i + j - z, 2 * j + i - x) + 4, 4)
            out[u] = r[:, j * 384 : j * 384 + 384].reshape(8, 48, 384)


def halves_kernel(place, *refs):
    amps, columns, outs = refs[:2], refs[2:4], refs[4:7]
    t_raw, l_cols, t_hi, t_lo, c_wide, t_sem, c_sem, out_sem = refs[7:]
    y, c = place[0], place[3]
    t_copies, c_copies = [], []
    for k in range(4):
        at_y = lax.rem(y + k, 4)
        for ref, core in zip(amps, (c, 1 - c)):
            target = t_raw.at[:, offset(lax.rem(at_y, 2), 48), offset(at_y // 2 * 2 + core, 384)]
            t_copies.append(pltpu.make_async_copy(ref.at[k], target, t_sem))
        for ref, core in zip(columns, (c, 1 - c)):
            c_copies.append(pltpu.make_async_copy(ref.at[k], l_cols.at[at_y, :, :, offset(core, 384)], c_sem))
    start(t_copies + c_copies)
    wait(t_copies)

    @pl.loop(0, 8)
    def _(i):
        t_hi[offset(i, 96), :], t_lo[offset(i, 96), :] = split(t_raw[i])

    wait(c_copies)

    @pl.loop(0, 4)
    def _(e):
        high, low = split(l_cols[e].reshape(384, 768))
        for k, part in enumerate((high, high, low)):
            c_wide[e, :, k * 768 : k * 768 + 768] = part

    copies = [pltpu.make_async_copy(ref, out, out_sem) for ref, out in zip((t_hi, t_lo, c_wide), outs)]
    start(copies)
    wait(copies)


def second_kernel(place, *refs):
    rows, (t_hi_in, t_lo_in, c_in), outs = refs[:5], refs[5:8], refs[8:11]
    l_rows, t_hi, t_lo, half, a_wide, c_wide, blocks, t_sem, row_sem, c_sem, out_sem = refs[11:]
    t_copies = [pltpu.make_async_copy(t_hi_in, t_hi, t_sem), pltpu.make_async_copy(t_lo_in, t_lo, t_sem)]
    r_copies = [row_copies(place, rows, l_rows, pl.ds(4 * q, 4), row_sem.at[q]) for q in range(2)]
    c_copies = [pltpu.make_async_copy(c_in, c_wide, c_sem)]
    start(t_copies + r_copies[0])
    wait(t_copies + r_copies[0])
    start(r_copies[1] + c_copies)
    for q in range(2):
        if q == 1:
            wait(r_copies[1])
        b = split(l_rows[4 * q : 4 * q + 4].reshape(768, 1536))
        for m in range(2):
            chunk = pl.ds(m * 384, 384)
            h = dot3((t_hi[chunk, :], t_lo[chunk, :]), b)
            for j in range(8):
                for p in range(4):
                    at = ((j % 2) * 8 + q * 4 + p) * 48
                    half[m * 4 + j // 2, at : at + 48, :] = h[j * 48 : j * 48 + 48, p * 192 : p * 192 + 192]

    @pl.loop(0, 8)
    def _(i):
        high, low = split(half[i].T)
        for k, part in enumerate((high, low, high)):
            for b in range(4):
                a_wide[b, offset(i, 48), k * 768 : k * 768 + 768] = part[b * 48 : b * 48 + 48, :]

    wait(c_copies)
    copies = [pltpu.make_async_copy(blocks.at[pl.ds(2 * k, 2)], outs[k], out_sem) for k in range(2)]
    copies.append(pltpu.make_async_copy(a_wide, outs[2], out_sem))
    start(copies[2:])
    ladder_of(place, 2, a_wide, c_wide, blocks)
    start(copies[:2])
    wait(copies)


def third_kernel(place, a_in, c_in, *refs):
    outs, (a_wide, c_wide, blocks, sem, out_sem) = refs[:4], refs[4:]
    held = [pltpu.make_async_copy(a_in, a_wide, sem), pltpu.make_async_copy(c_in, c_wide, sem)]
    start(held)
    wait(held)
    copies = [pltpu.make_async_copy(blocks.at[k // 2, pl.ds(k % 2 * 2, 2)], out, out_sem) for k, out in enumerate(outs)]
    for k, v in enumerate((1, 3)):
        ladder_of(place, v, a_wide, c_wide, blocks.at[k])
        start(copies[2 * k : 2 * k + 2])
    wait(copies)


def fourth_kernel(place, a_in, c_in, b1, d0, out, a_wide, c_wide, sem):
    del b1, d0
    held = [pltpu.make_async_copy(a_in, a_wide, sem), pltpu.make_async_copy(c_in, c_wide, sem)]
    start(held)
    wait(held)
    ladder_of(place, 0, a_wide, c_wide, out)


ANYWHERE = pl.BlockSpec(memory_space=pl.ANY)
ON_HBM = pl.BlockSpec(memory_space=pltpu.HBM)
ON_SMEM = pl.BlockSpec(memory_space=pltpu.SMEM)
ON_VMEM = pl.BlockSpec(memory_space=pltpu.VMEM)
DMA = pltpu.SemaphoreType.DMA
QUAD = jax.ShapeDtypeStruct((4, 8, 48, 384), F32)
PAIR = jax.ShapeDtypeStruct((2, 8, 48, 384), F32)
WIDE = jax.ShapeDtypeStruct((4, 384, 2304), BF16)


AMPS = (768, 1536)
HALF_AMPS = jax.ShapeDtypeStruct(AMPS, BF16)


def call(body, out_shape, out_spec, scratch, megabytes, units, place, *args):
    return pl.pallas_call(
        body,
        out_shape=out_shape,
        in_specs=[ON_SMEM] + [ANYWHERE] * len(args),
        out_specs=[out_spec] * len(out_shape),
        scratch_shapes=scratch,
        compiler_params=pltpu.CompilerParams(vmem_limit_bytes=megabytes << 20),
        cost_estimate=pl.CostEstimate(flops=units * 3 * 905969664, bytes_accessed=12 << 20, transcendentals=0),
    )(place, *args)


def halves(place, amps, columns):
    scratch = [pltpu.VMEM((8, 96, 1536), F32), pltpu.VMEM((4, 8, 48, 768), F32)]
    scratch += [pltpu.VMEM(AMPS, BF16)] * 2 + [pltpu.VMEM(WIDE.shape, BF16)] + [DMA] * 3
    return call(halves_kernel, [HALF_AMPS] * 2 + [WIDE], ON_HBM, scratch, 28, 1, place, *amps, *columns)


def second(place, rows, parts):
    scratch = [pltpu.VMEM((8, 192, 1536), F32)] + [pltpu.VMEM(AMPS, BF16)] * 2 + [pltpu.VMEM((8, 768, 192), F32)]
    scratch += [pltpu.VMEM(WIDE.shape, BF16)] * 2 + [pltpu.VMEM(QUAD.shape, F32)]
    scratch += [DMA, DMA((2,)), DMA, DMA]
    return call(second_kernel, [PAIR] * 2 + [WIDE], ON_HBM, scratch, 48, 5, place, *rows, *parts)


def third(place, parts):
    scratch = [pltpu.VMEM(WIDE.shape, BF16)] * 2 + [pltpu.VMEM((2, *QUAD.shape), F32), DMA, DMA]
    return call(third_kernel, [PAIR] * 4, ON_HBM, scratch, 32, 2, place, *parts)


def fourth(place, parts, after):
    scratch = [pltpu.VMEM(WIDE.shape, BF16)] * 2 + [DMA]
    return call(fourth_kernel, [QUAD], ON_VMEM, scratch, 28, 1, place, *parts, *after)[0]


def shuffle(cholesky, after):
    return pl.pallas_call(
        shuffle_kernel,
        out_shape=jax.ShapeDtypeStruct((8, 48, 384), F32),
        in_specs=[ON_VMEM, ANYWHERE],
        out_specs=ON_VMEM,
        compiler_params=pltpu.CompilerParams(vmem_limit_bytes=8 << 20),
    )(cholesky, after)


def body(cholesky, amplitudes):
    y, xl, z, xh, c = (lax.axis_index(axis) for axis in AXES)
    place = jnp.stack([y, z, 2 * xh + xl, c]).astype(jnp.int32)

    def from_plus(value):
        return permute(value, lambda *at: far(at, -1))

    def from_minus(value):
        return permute(value, lambda *at: far(at, 1))

    mine = permute(cholesky, lambda *at: swapped(at))
    near_rows = [mine] + [permute(mine, lambda *at, u=u: near(at, -u)) for u in (1, 2, 3)]

    own_t = permute(amplitudes, lambda y, xl, z, xh, c: (2 * xh + y % 2, xl, z, y // 2, c))
    own_c = lax.all_to_all(shuffle(cholesky, mine), ("xl", "z"), 0, 0, tiled=True)

    def from_y(value, by):
        return permute(value, lambda *at: shift_y(at, -by))

    def round_y(own):
        p, m = from_y(own, 1), from_y(own, -1)
        far_one = jnp.concatenate([from_y(p[:4], 1), from_y(m[4:], -1)])
        ring = jnp.stack([own, p, far_one, m])
        return ring, permute(ring, other_core)

    amps, cols = round_y(own_t), round_y(own_c)

    s = jnp.stack(near_rows)
    p, m = from_plus(s), from_minus(s)
    rows = (s, p, m, from_plus(p[:2]), from_minus(m[2:]))

    t_hi, t_lo, c_wide = halves(place, amps, cols)
    r2a, r2b, a_wide = second(place, rows, (t_hi, t_lo, c_wide))
    r1a, r1b, r3a, r3b = third(place, (a_wide, c_wide))

    def to_plus(value):
        return permute(value, lambda *at: far(at, 1))

    def to_minus(value):
        return permute(value, lambda *at: far(at, -1))

    a0, a1 = to_plus(r2a), to_minus(r2b)
    b1, d0 = to_plus(r1b), to_minus(r3a)
    r0 = fourth(place, (a_wide, c_wide), (b1, d0))
    b0, d1 = to_plus(r1a + a0), to_minus(r3b + a1)
    q = (r0[:2] + b0 + d0, r0[2:] + b1 + d1)
    got = [permute(q[u // 2][u % 2], lambda *at, u=u: near(at, u)) for u in (1, 2, 3)]
    total = (q[0][0] + got[0]) + (got[1] + got[2])
    return permute(total, lambda *at: swapped(at)).transpose(0, 2, 1)


def solution(mesh):
    fine = Mesh(mesh.devices.reshape(SIZES), AXES)
    split_in = P(None, ("y", "xl", "z"), ("xh", "c"))
    return jax.shard_map(
        body, mesh=fine, in_specs=(split_in, split_in), out_specs=P(None, ("xh", "c"), ("y", "xl", "z")), check_vma=False
    )
```

```python
import functools

import jax
import jax.numpy as jnp
from jax import lax
from jax.experimental import pallas as pl
from jax.experimental.pallas import tpu as pltpu
from jax.sharding import Mesh
from jax.sharding import PartitionSpec as P

AXES = ("y", "xl", "z", "xh", "c")
SIZES = (4, 2, 4, 2, 2)
F32, BF16 = jnp.float32, jnp.bfloat16


def coords(index):
    out = []
    for size in reversed(SIZES):
        out.append(index % size)
        index //= size
    return tuple(reversed(out))


def index_of(at):
    index = 0
    for size, value in zip(SIZES, at):
        index = index * size + value
    return index


def permute(value, target):
    pairs = [(s, index_of(target(*coords(s)))) for s in range(128)]
    return lax.ppermute(value, AXES, pairs)


def shift_x(at, by):
    y, xl, z, xh, c = at
    x = (2 * xh + xl + by) % 4
    return (y, x % 2, z, x // 2, c)


def shift_z(at, by):
    y, xl, z, xh, c = at
    return (y, xl, (z + by) % 4, xh, c)


def shift_y(at, by):
    y, xl, z, xh, c = at
    return ((y + by) % 4, xl, z, xh, c)


def near(at, by):
    return shift_z(at, by) if at[4] == 0 else shift_x(at, by)


def far(at, by):
    return shift_x(at, by) if at[4] == 0 else shift_z(at, by)


def swapped(at):
    y, xl, z, xh, c = at
    return (y, xl, z // 2 * 2 + c, xh, z % 2)


def other_core(*at):
    return at[:4] + (1 - at[4],)


def split(value):
    high = value.astype(BF16)
    return high, (value - high.astype(F32)).astype(BF16)


def times(a, b):
    return lax.dot_general(a, b, (((1,), (1,)), ((), ())), preferred_element_type=F32)


def dot3(a, b):
    return times(a[0], b[0]) + (times(a[0], b[1]) + times(a[1], b[0]))


def offset(value, size):
    return pl.ds(pl.multiple_of(value * size, size), size)


def row_copies(place, refs, target, vectors, sem):
    z, x, c = place[1], place[2], place[3]
    copies = []
    for ref, v, us in zip(refs, (0, 1, 3, 2, 2), (range(4), range(4), range(4), range(2), range(2, 4))):
        for k, u in enumerate(us):
            at_z = lax.rem(z + jnp.where(c == 0, u, v), 4)
            at_x = lax.rem(x + jnp.where(c == 0, v, u), 4)
            b, d = lax.rem(at_x, 2) * 2 + at_z // 2, at_x // 2 * 2 + lax.rem(at_z, 2)
            copies.append(pltpu.make_async_copy(ref.at[k, vectors], target.at[vectors, offset(b, 48), offset(d, 384)], sem))
    return copies


def shuffle_kernel(l_ref, after, out):
    del after
    for m in range(8):
        out[m] = jnp.concatenate([l_ref[p][:, m * 48 : m * 48 + 48] for p in range(8)], axis=1)


def start(copies):
    for copy in copies:
        copy.start()


def wait(copies):
    for copy in copies:
        copy.wait()


def ladder_of(place, v, a_wide, c_wide, out):
    z, x, c = place[1], place[2], place[3]
    at_z, at_x = lax.rem(z + v, 4), lax.rem(x + v, 4)
    columns = [jnp.where(c == 0, at_x // 2 * 2 + j, lax.rem(at_z, 2) + 2 * j) for j in range(2)]
    for i in range(2):
        b = jnp.where(c == 0, lax.rem(at_x, 2) * 2 + i, at_z // 2 + 2 * i)
        r = times(a_wide[b], jnp.concatenate([c_wide[at] for at in columns]))
        for j in range(2):
            u = lax.rem(jnp.where(c == 0, 2 * i + j - z, 2 * j + i - x) + 4, 4)
            out[u] = r[:, j * 384 : j * 384 + 384].reshape(8, 48, 384)


def halves_kernel(place, *refs):
    amps, columns, outs = refs[:2], refs[2:4], refs[4:7]
    t_raw, l_cols, t_hi, t_lo, c_wide, t_sem, c_sem, out_sem = refs[7:]
    y, c = place[0], place[3]
    t_copies, c_copies = [], []
    for k in range(4):
        at_y = lax.rem(y + k, 4)
        for ref, core in zip(amps, (c, 1 - c)):
            target = t_raw.at[:, offset(lax.rem(at_y, 2), 48), offset(at_y // 2 * 2 + core, 384)]
            t_copies.append(pltpu.make_async_copy(ref.at[k], target, t_sem))
        for ref, core in zip(columns, (c, 1 - c)):
            c_copies.append(pltpu.make_async_copy(ref.at[k], l_cols.at[at_y, :, :, offset(core, 384)], c_sem))
    start(t_copies + c_copies)
    wait(t_copies)

    @pl.loop(0, 8)
    def _(i):
        t_hi[offset(i, 96), :], t_lo[offset(i, 96), :] = split(t_raw[i])

    wait(c_copies)

    @pl.loop(0, 4)
    def _(e):
        high, low = split(l_cols[e].reshape(384, 768))
        for k, part in enumerate((high, high, low)):
            c_wide[e, :, k * 768 : k * 768 + 768] = part

    copies = [pltpu.make_async_copy(ref, out, out_sem) for ref, out in zip((t_hi, t_lo, c_wide), outs)]
    start(copies)
    wait(copies)


def second_kernel(place, *refs):
    rows, (t_hi_in, t_lo_in, c_in), outs = refs[:5], refs[5:8], refs[8:11]
    l_rows, t_hi, t_lo, half, a_wide, c_wide, blocks, t_sem, row_sem, c_sem, out_sem = refs[11:]
    t_copies = [pltpu.make_async_copy(t_hi_in, t_hi, t_sem), pltpu.make_async_copy(t_lo_in, t_lo, t_sem)]
    r_copies = [row_copies(place, rows, l_rows, pl.ds(4 * q, 4), row_sem.at[q]) for q in range(2)]
    c_copies = [pltpu.make_async_copy(c_in, c_wide, c_sem)]
    start(t_copies + r_copies[0])
    wait(t_copies + r_copies[0])
    start(r_copies[1] + c_copies)
    for q in range(2):
        if q == 1:
            wait(r_copies[1])
        b = split(l_rows[4 * q : 4 * q + 4].reshape(768, 1536))
        for m in range(2):
            chunk = pl.ds(m * 384, 384)
            h = dot3((t_hi[chunk, :], t_lo[chunk, :]), b)
            for j in range(8):
                for p in range(4):
                    at = ((j % 2) * 8 + q * 4 + p) * 48
                    half[m * 4 + j // 2, at : at + 48, :] = h[j * 48 : j * 48 + 48, p * 192 : p * 192 + 192]

    for i in range(8):
        high, low = split(half[i].T)
        for k, part in enumerate((high, low, high)):
            for b in range(4):
                a_wide[b, i * 48 : i * 48 + 48, k * 768 : k * 768 + 768] = part[b * 48 : b * 48 + 48, :]

    wait(c_copies)
    copies = [pltpu.make_async_copy(blocks.at[pl.ds(2 * k, 2)], outs[k], out_sem) for k in range(2)]
    copies.append(pltpu.make_async_copy(a_wide.at[:, :, pl.ds(0, 1536)], outs[2], out_sem))
    start(copies[2:])
    ladder_of(place, 2, a_wide, c_wide, blocks)
    start(copies[:2])
    wait(copies)


def held_copies(a_in, c_in, a_wide, c_wide, sem):
    return [
        pltpu.make_async_copy(a_in, a_wide.at[:, :, pl.ds(0, 1536)], sem),
        pltpu.make_async_copy(a_in.at[:, :, pl.ds(0, 768)], a_wide.at[:, :, pl.ds(1536, 768)], sem),
        pltpu.make_async_copy(c_in, c_wide, sem),
    ]


def third_kernel(place, a_in, c_in, *refs):
    outs, (a_wide, c_wide, blocks, sem, out_sem) = refs[:4], refs[4:]
    held = held_copies(a_in, c_in, a_wide, c_wide, sem)
    start(held)
    wait(held)
    copies = [pltpu.make_async_copy(blocks.at[k // 2, pl.ds(k % 2 * 2, 2)], out, out_sem) for k, out in enumerate(outs)]
    for k, v in enumerate((1, 3)):
        ladder_of(place, v, a_wide, c_wide, blocks.at[k])
        start(copies[2 * k : 2 * k + 2])
    wait(copies)


def fourth_kernel(place, a_in, c_in, b1, d0, out, a_wide, c_wide, sem):
    del b1, d0
    held = held_copies(a_in, c_in, a_wide, c_wide, sem)
    start(held)
    wait(held)
    ladder_of(place, 0, a_wide, c_wide, out)


ANYWHERE = pl.BlockSpec(memory_space=pl.ANY)
ON_HBM = pl.BlockSpec(memory_space=pltpu.HBM)
ON_SMEM = pl.BlockSpec(memory_space=pltpu.SMEM)
ON_VMEM = pl.BlockSpec(memory_space=pltpu.VMEM)
DMA = pltpu.SemaphoreType.DMA
QUAD = jax.ShapeDtypeStruct((4, 8, 48, 384), F32)
PAIR = jax.ShapeDtypeStruct((2, 8, 48, 384), F32)
WIDE = jax.ShapeDtypeStruct((4, 384, 2304), BF16)
BOTH = jax.ShapeDtypeStruct((4, 384, 1536), BF16)


AMPS = (768, 1536)
HALF_AMPS = jax.ShapeDtypeStruct(AMPS, BF16)


def call(body, out_shape, out_spec, scratch, megabytes, units, place, *args, in_hbm=0):
    return pl.pallas_call(
        body,
        out_shape=out_shape,
        in_specs=[ON_SMEM] + [ON_HBM] * in_hbm + [ANYWHERE] * (len(args) - in_hbm),
        out_specs=[out_spec] * len(out_shape),
        scratch_shapes=scratch,
        compiler_params=pltpu.CompilerParams(vmem_limit_bytes=megabytes << 20),
        cost_estimate=pl.CostEstimate(flops=units * 3 * 905969664, bytes_accessed=12 << 20, transcendentals=0),
    )(place, *args)


def halves(place, amps, columns):
    scratch = [pltpu.VMEM((8, 96, 1536), F32), pltpu.VMEM((4, 8, 48, 768), F32)]
    scratch += [pltpu.VMEM(AMPS, BF16)] * 2 + [pltpu.VMEM(WIDE.shape, BF16)] + [DMA] * 3
    return call(halves_kernel, [HALF_AMPS] * 2 + [WIDE], ON_HBM, scratch, 28, 1, place, *amps, *columns)


def second(place, rows, parts):
    scratch = [pltpu.VMEM((8, 192, 1536), F32)] + [pltpu.VMEM(AMPS, BF16)] * 2 + [pltpu.VMEM((8, 768, 192), F32)]
    scratch += [pltpu.VMEM(WIDE.shape, BF16)] * 2 + [pltpu.VMEM(QUAD.shape, F32)]
    scratch += [DMA, DMA((2,)), DMA, DMA]
    return call(second_kernel, [PAIR] * 2 + [BOTH], ON_HBM, scratch, 48, 5, place, *rows, *parts)


def third(place, parts):
    scratch = [pltpu.VMEM(WIDE.shape, BF16)] * 2 + [pltpu.VMEM((2, *QUAD.shape), F32), DMA, DMA]
    return call(third_kernel, [PAIR] * 4, ON_HBM, scratch, 32, 2, place, *parts, in_hbm=2)


def fourth(place, parts, after):
    scratch = [pltpu.VMEM(WIDE.shape, BF16)] * 2 + [DMA]
    return call(fourth_kernel, [QUAD], ON_VMEM, scratch, 28, 1, place, *parts, *after, in_hbm=2)[0]


def shuffle(cholesky, after):
    return pl.pallas_call(
        shuffle_kernel,
        out_shape=jax.ShapeDtypeStruct((8, 48, 384), F32),
        in_specs=[ON_VMEM, ANYWHERE],
        out_specs=ON_VMEM,
        compiler_params=pltpu.CompilerParams(vmem_limit_bytes=8 << 20),
    )(cholesky, after)


def body(cholesky, amplitudes):
    y, xl, z, xh, c = (lax.axis_index(axis) for axis in AXES)
    place = jnp.stack([y, z, 2 * xh + xl, c]).astype(jnp.int32)

    def from_plus(value):
        return permute(value, lambda *at: far(at, -1))

    def from_minus(value):
        return permute(value, lambda *at: far(at, 1))

    mine = permute(cholesky, lambda *at: swapped(at))
    near_rows = [mine] + [permute(mine, lambda *at, u=u: near(at, -u)) for u in (1, 2, 3)]

    own_t = permute(amplitudes, lambda y, xl, z, xh, c: (2 * xh + y % 2, xl, z, y // 2, c))
    own_c = lax.all_to_all(shuffle(cholesky, mine), ("xl", "z"), 0, 0, tiled=True)

    def from_y(value, by):
        return permute(value, lambda *at: shift_y(at, -by))

    def round_y(own):
        p, m = from_y(own, 1), from_y(own, -1)
        far_one = jnp.concatenate([from_y(p[:4], 1), from_y(m[4:], -1)])
        ring = jnp.stack([own, p, far_one, m])
        return ring, permute(ring, other_core)

    amps, cols = round_y(own_t), round_y(own_c)

    s = jnp.stack(near_rows)
    p, m = from_plus(s), from_minus(s)
    rows = (s, p, m, from_plus(p[:2]), from_minus(m[2:]))

    t_hi, t_lo, c_wide = halves(place, amps, cols)
    r2a, r2b, a_both = second(place, rows, (t_hi, t_lo, c_wide))
    r1a, r1b, r3a, r3b = third(place, (a_both, c_wide))

    def to_plus(value):
        return permute(value, lambda *at: far(at, 1))

    def to_minus(value):
        return permute(value, lambda *at: far(at, -1))

    a0, a1 = to_plus(r2a), to_minus(r2b)
    b1, d0 = to_plus(r1b), to_minus(r3a)
    r0 = fourth(place, (a_both, c_wide), (b1, d0))
    b0, d1 = to_plus(r1a + a0), to_minus(r3b + a1)
    q = (r0[:2] + b0 + d0, r0[2:] + b1 + d1)
    got = [permute(q[u // 2][u % 2], lambda *at, u=u: near(at, u)) for u in (3, 2, 1)]
    total = (q[0][0] + got[0]) + (got[1] + got[2])
    return permute(total, lambda *at: swapped(at)).transpose(0, 2, 1)


def solution(mesh):
    fine = Mesh(mesh.devices.reshape(SIZES), AXES)
    split_in = P(None, ("y", "xl", "z"), ("xh", "c"))
    return jax.shard_map(
        body, mesh=fine, in_specs=(split_in, split_in), out_specs=P(None, ("xh", "c"), ("y", "xl", "z")), check_vma=False
    )
```

```python
import functools

import jax
import jax.numpy as jnp
from jax import lax
from jax.experimental import pallas as pl
from jax.experimental.pallas import tpu as pltpu
from jax.sharding import Mesh
from jax.sharding import PartitionSpec as P

AXES = ("y", "xl", "z", "xh", "c")
SIZES = (4, 2, 4, 2, 2)
F32, BF16 = jnp.float32, jnp.bfloat16


def coords(index):
    out = []
    for size in reversed(SIZES):
        out.append(index % size)
        index //= size
    return tuple(reversed(out))


def index_of(at):
    index = 0
    for size, value in zip(SIZES, at):
        index = index * size + value
    return index


def permute(value, target):
    pairs = [(s, index_of(target(*coords(s)))) for s in range(128)]
    return lax.ppermute(value, AXES, pairs)


def shift_x(at, by):
    y, xl, z, xh, c = at
    x = (2 * xh + xl + by) % 4
    return (y, x % 2, z, x // 2, c)


def shift_z(at, by):
    y, xl, z, xh, c = at
    return (y, xl, (z + by) % 4, xh, c)


def shift_y(at, by):
    y, xl, z, xh, c = at
    return ((y + by) % 4, xl, z, xh, c)


def near(at, by):
    return shift_z(at, by) if at[4] == 0 else shift_x(at, by)


def far(at, by):
    return shift_x(at, by) if at[4] == 0 else shift_z(at, by)


def swapped(at):
    y, xl, z, xh, c = at
    return (y, xl, z // 2 * 2 + c, xh, z % 2)


def other_core(*at):
    return at[:4] + (1 - at[4],)


def split(value):
    high = value.astype(BF16)
    return high, (value - high.astype(F32)).astype(BF16)


def times(a, b):
    return lax.dot_general(a, b, (((1,), (1,)), ((), ())), preferred_element_type=F32)


def dot3(a, b):
    return times(a[0], b[0]) + (times(a[0], b[1]) + times(a[1], b[0]))


def offset(value, size):
    return pl.ds(pl.multiple_of(value * size, size), size)


def row_copies(place, refs, target, vectors, sem):
    z, x, c = place[1], place[2], place[3]
    copies = []
    for ref, v, us in zip(refs, (0, 1, 3, 2, 2), (range(4), range(4), range(4), range(2), range(2, 4))):
        for k, u in enumerate(us):
            at_z = lax.rem(z + jnp.where(c == 0, u, v), 4)
            at_x = lax.rem(x + jnp.where(c == 0, v, u), 4)
            b, d = lax.rem(at_x, 2) * 2 + at_z // 2, at_x // 2 * 2 + lax.rem(at_z, 2)
            copies.append(pltpu.make_async_copy(ref.at[k, vectors], target.at[vectors, offset(b, 48), offset(d, 384)], sem))
    return copies


def shuffle_kernel(l_ref, after, out):
    del after
    for m in range(8):
        out[m] = jnp.concatenate([l_ref[p][:, m * 48 : m * 48 + 48] for p in range(8)], axis=1)


def start(copies):
    for copy in copies:
        copy.start()


def wait(copies):
    for copy in copies:
        copy.wait()


def ladder_of(place, v, a_wide, c_wide, out):
    z, x, c = place[1], place[2], place[3]
    at_z, at_x = lax.rem(z + v, 4), lax.rem(x + v, 4)
    columns = [jnp.where(c == 0, at_x // 2 * 2 + j, lax.rem(at_z, 2) + 2 * j) for j in range(2)]
    for i in range(2):
        b = jnp.where(c == 0, lax.rem(at_x, 2) * 2 + i, at_z // 2 + 2 * i)
        r = times(a_wide[b], jnp.concatenate([c_wide[at] for at in columns]))
        for j in range(2):
            u = lax.rem(jnp.where(c == 0, 2 * i + j - z, 2 * j + i - x) + 4, 4)
            out[u] = r[:, j * 384 : j * 384 + 384].reshape(8, 48, 384)


def halves_kernel(place, *refs):
    amps, columns, outs = refs[:2], refs[2:4], refs[4:7]
    t_raw, l_cols, t_hi, t_lo, c_wide, t_sem, c_sem, out_sem = refs[7:]
    y, c = place[0], place[3]
    t_copies, c_copies = [], []
    for k in range(4):
        at_y = lax.rem(y + k, 4)
        for ref, core in zip(amps, (c, 1 - c)):
            target = t_raw.at[:, offset(lax.rem(at_y, 2), 48), offset(at_y // 2 * 2 + core, 384)]
            t_copies.append(pltpu.make_async_copy(ref.at[k], target, t_sem))
        for ref, core in zip(columns, (c, 1 - c)):
            c_copies.append(pltpu.make_async_copy(ref.at[k], l_cols.at[at_y, :, :, offset(core, 384)], c_sem))
    start(t_copies + c_copies)
    wait(t_copies)

    @pl.loop(0, 8)
    def _(i):
        t_hi[offset(i, 96), :], t_lo[offset(i, 96), :] = split(t_raw[i])

    wait(c_copies)

    @pl.loop(0, 4)
    def _(e):
        high, low = split(l_cols[e].reshape(384, 768))
        for k, part in enumerate((high, high, low)):
            c_wide[e, :, k * 768 : k * 768 + 768] = part

    copies = [pltpu.make_async_copy(ref, out, out_sem) for ref, out in zip((t_hi, t_lo, c_wide), outs)]
    start(copies)
    wait(copies)


def second_kernel(place, *refs):
    (t_hi, t_lo, c_wide), rows, outs = refs[:3], refs[3:8], refs[8:11]
    l_rows, half, a_wide, blocks, row_sem, out_sem = refs[11:]
    r_copies = [row_copies(place, rows, l_rows, pl.ds(4 * q, 4), row_sem.at[q]) for q in range(2)]
    start(r_copies[0])
    wait(r_copies[0])
    start(r_copies[1])
    for q in range(2):
        if q == 1:
            wait(r_copies[1])
        b = split(l_rows[4 * q : 4 * q + 4].reshape(768, 1536))
        for m in range(2):
            chunk = pl.ds(m * 384, 384)
            h = dot3((t_hi[chunk, :], t_lo[chunk, :]), b)
            for j in range(8):
                for p in range(4):
                    at = ((j % 2) * 8 + q * 4 + p) * 48
                    half[m * 4 + j // 2, at : at + 48, :] = h[j * 48 : j * 48 + 48, p * 192 : p * 192 + 192]

    for i in range(8):
        high, low = split(half[i].T)
        for k, part in enumerate((high, low, high)):
            for b in range(4):
                a_wide[b, i * 48 : i * 48 + 48, k * 768 : k * 768 + 768] = part[b * 48 : b * 48 + 48, :]

    copies = [pltpu.make_async_copy(blocks.at[pl.ds(2 * k, 2)], outs[k], out_sem) for k in range(2)]
    copies.append(pltpu.make_async_copy(a_wide.at[:, :, pl.ds(0, 1536)], outs[2], out_sem))
    start(copies[2:])
    ladder_of(place, 2, a_wide, c_wide, blocks)
    start(copies[:2])
    wait(copies)


def held_copies(a_in, c_in, a_wide, c_wide, sem):
    return [
        pltpu.make_async_copy(a_in, a_wide.at[:, :, pl.ds(0, 1536)], sem),
        pltpu.make_async_copy(a_in.at[:, :, pl.ds(0, 768)], a_wide.at[:, :, pl.ds(1536, 768)], sem),
        pltpu.make_async_copy(c_in, c_wide, sem),
    ]


def third_kernel(place, a_in, c_in, *refs):
    outs, (a_wide, c_wide, blocks, sem, out_sem) = refs[:4], refs[4:]
    held = held_copies(a_in, c_in, a_wide, c_wide, sem)
    start(held)
    wait(held)
    copies = [pltpu.make_async_copy(blocks.at[k // 2, pl.ds(k % 2 * 2, 2)], out, out_sem) for k, out in enumerate(outs)]
    for k, v in enumerate((1, 3)):
        ladder_of(place, v, a_wide, c_wide, blocks.at[k])
        start(copies[2 * k : 2 * k + 2])
    wait(copies)


def fourth_kernel(place, a_in, c_in, b1, d0, out, a_wide, c_wide, sem):
    del b1, d0
    held = held_copies(a_in, c_in, a_wide, c_wide, sem)
    start(held)
    wait(held)
    ladder_of(place, 0, a_wide, c_wide, out)


ANYWHERE = pl.BlockSpec(memory_space=pl.ANY)
ON_HBM = pl.BlockSpec(memory_space=pltpu.HBM)
ON_SMEM = pl.BlockSpec(memory_space=pltpu.SMEM)
ON_VMEM = pl.BlockSpec(memory_space=pltpu.VMEM)
DMA = pltpu.SemaphoreType.DMA
QUAD = jax.ShapeDtypeStruct((4, 8, 48, 384), F32)
PAIR = jax.ShapeDtypeStruct((2, 8, 48, 384), F32)
WIDE = jax.ShapeDtypeStruct((4, 384, 2304), BF16)
BOTH = jax.ShapeDtypeStruct((4, 384, 1536), BF16)


AMPS = (768, 1536)
HALF_AMPS = jax.ShapeDtypeStruct(AMPS, BF16)


def call(body, out_shape, out_spec, scratch, megabytes, units, place, *args, in_hbm=0, in_vmem=0):
    return pl.pallas_call(
        body,
        out_shape=out_shape,
        in_specs=[ON_SMEM] + [ON_VMEM] * in_vmem + [ON_HBM] * in_hbm + [ANYWHERE] * (len(args) - in_hbm - in_vmem),
        out_specs=[out_spec] * len(out_shape),
        scratch_shapes=scratch,
        compiler_params=pltpu.CompilerParams(vmem_limit_bytes=megabytes << 20),
        cost_estimate=pl.CostEstimate(flops=units * 3 * 905969664, bytes_accessed=12 << 20, transcendentals=0),
    )(place, *args)


def halves(place, amps, columns):
    scratch = [pltpu.VMEM((8, 96, 1536), F32), pltpu.VMEM((4, 8, 48, 768), F32)]
    scratch += [pltpu.VMEM(AMPS, BF16)] * 2 + [pltpu.VMEM(WIDE.shape, BF16)] + [DMA] * 3
    return call(halves_kernel, [HALF_AMPS] * 2 + [WIDE], ON_HBM, scratch, 28, 1, place, *amps, *columns)


def second(place, rows, parts):
    scratch = [pltpu.VMEM((8, 192, 1536), F32), pltpu.VMEM((8, 768, 192), F32)]
    scratch += [pltpu.VMEM(WIDE.shape, BF16), pltpu.VMEM(QUAD.shape, F32), DMA((2,)), DMA]
    return call(second_kernel, [PAIR] * 2 + [BOTH], ON_HBM, scratch, 40, 5, place, *parts, *rows, in_vmem=3)


def third(place, parts):
    scratch = [pltpu.VMEM(WIDE.shape, BF16)] * 2 + [pltpu.VMEM((2, *QUAD.shape), F32), DMA, DMA]
    return call(third_kernel, [PAIR] * 4, ON_HBM, scratch, 32, 2, place, *parts, in_hbm=2)


def fourth(place, parts, after):
    scratch = [pltpu.VMEM(WIDE.shape, BF16)] * 2 + [DMA]
    return call(fourth_kernel, [QUAD], ON_VMEM, scratch, 28, 1, place, *parts, *after, in_hbm=2)[0]


def shuffle(cholesky, after):
    return pl.pallas_call(
        shuffle_kernel,
        out_shape=jax.ShapeDtypeStruct((8, 48, 384), F32),
        in_specs=[ON_VMEM, ANYWHERE],
        out_specs=ON_VMEM,
        compiler_params=pltpu.CompilerParams(vmem_limit_bytes=8 << 20),
    )(cholesky, after)


def body(cholesky, amplitudes):
    y, xl, z, xh, c = (lax.axis_index(axis) for axis in AXES)
    place = jnp.stack([y, z, 2 * xh + xl, c]).astype(jnp.int32)

    def from_plus(value):
        return permute(value, lambda *at: far(at, -1))

    def from_minus(value):
        return permute(value, lambda *at: far(at, 1))

    mine = permute(cholesky, lambda *at: swapped(at))
    near_rows = [mine] + [permute(mine, lambda *at, u=u: near(at, -u)) for u in (1, 2, 3)]

    own_t = permute(amplitudes, lambda y, xl, z, xh, c: (2 * xh + y % 2, xl, z, y // 2, c))
    own_c = lax.all_to_all(shuffle(cholesky, mine), ("xl", "z"), 0, 0, tiled=True)

    def from_y(value, by):
        return permute(value, lambda *at: shift_y(at, -by))

    def round_y(own):
        p, m = from_y(own, 1), from_y(own, -1)
        far_one = jnp.concatenate([from_y(p[:4], 1), from_y(m[4:], -1)])
        ring = jnp.stack([own, p, far_one, m])
        return ring, permute(ring, other_core)

    amps, cols = round_y(own_t), round_y(own_c)

    s = jnp.stack(near_rows)
    p, m = from_plus(s), from_minus(s)
    rows = (s, p, m, from_plus(p[:2]), from_minus(m[2:]))

    t_hi, t_lo, c_wide = halves(place, amps, cols)
    r2a, r2b, a_both = second(place, rows, (t_hi, t_lo, c_wide))
    r1a, r1b, r3a, r3b = third(place, (a_both, c_wide))

    def to_plus(value):
        return permute(value, lambda *at: far(at, 1))

    def to_minus(value):
        return permute(value, lambda *at: far(at, -1))

    a0, a1 = to_plus(r2a), to_minus(r2b)
    b1, d0 = to_plus(r1b), to_minus(r3a)
    r0 = fourth(place, (a_both, c_wide), (b1, d0))
    b0, d1 = to_plus(r1a + a0), to_minus(r3b + a1)
    q = (r0[:2] + b0 + d0, r0[2:] + b1 + d1)
    got = [permute(q[u // 2][u % 2], lambda *at, u=u: near(at, u)) for u in (3, 2, 1)]
    total = (q[0][0] + got[0]) + (got[1] + got[2])
    return permute(total, lambda *at: swapped(at)).transpose(0, 2, 1)


def solution(mesh):
    fine = Mesh(mesh.devices.reshape(SIZES), AXES)
    split_in = P(None, ("y", "xl", "z"), ("xh", "c"))
    return jax.shard_map(
        body, mesh=fine, in_specs=(split_in, split_in), out_specs=P(None, ("xh", "c"), ("y", "xl", "z")), check_vma=False
    )
```
